32 devices in a mesh: replica: 8 (over z, core), expert: 4 (over y, x).
Axes of the slice: x: 2, y: 2, z: 4, core: 2. Of those that a mesh axis runs over, the one named last changes fastest.
Arguments:
- tokens: bfloat16 [4096, 2048], P(('replica', 'expert')), may hold values from -6 to 6
- cotangent: bfloat16 [4096, 2048], P(('replica', 'expert')), may hold values from -6 to 6
- routes: int32 [4096, 2], P(('replica', 'expert')), may hold values from 0 to 3, as said below
- slot_index: int32 [4096, 2], P(('replica', 'expert')), may hold values from 0 to 127, as said below
- route_weights: float32 [4096, 2], P(('replica', 'expert')), may hold values from 0.05 to 1
- gate_weight: bfloat16 [8, 4, 2048, 512], P('replica', 'expert'), may hold values from -0.125 to 0.125
- up_weight: bfloat16 [8, 4, 2048, 512], P('replica', 'expert'), may hold values from -0.125 to 0.125
- down_weight: bfloat16 [8, 4, 512, 2048], P('replica', 'expert'), may hold values from -0.25 to 0.25
- moment_first: float32 [8, 4, 512, 2048], P('replica', 'expert'), may hold values from -6 to 6
- moment_second: float32 [8, 4, 512, 2048], P('replica', 'expert'), may hold values from 0.5 to 20
- step_count: int32 [], replicated, may hold values from 0 to 999
Outputs:
- token_grad: bfloat16 [4096, 2048], P(('replica', 'expert'))
- route_grad: float32 [4096, 2], P(('replica', 'expert'))
- new_down: bfloat16 [8, 4, 512, 2048], P('replica', 'expert')
- new_first: float32 [8, 4, 512, 2048], P('replica', 'expert')
- new_second: float32 [8, 4, 512, 2048], P('replica', 'expert')
The draws below stay inside these ranges and needn't reach their ends.
Inputs may be any that keep to these rules, and one draw needn't show every extreme that they name: `routes`: each token names 2 different experts. Among the 128 tokens of one device each expert is named at most 128 times; one expert, the same for all devices of a replica, is named exactly 128 times on each of them, and the other experts are named equally often up to one. `slot_index`: routes of one device to one expert have different slots.
All inputs are finite; a program needn't handle non-finite values.
Results may differ from the reference program's by a relative error of at most 0.0065.
Values may be sent and summed in bfloat16 or wider, within the bound.
A program may use at most 128 MiB of HBM per device.

```python
import math
import jax
import jax.numpy as jnp
from jax import lax

D = 2048
FF = 512
TOK_DEV = 128
TOPK = 2
EXPERTS = 4
CAP = 128
TOKENS = 4096
N_REPLICA = 8
N_EXPERT = 4


def block_table(block_key, favored):
    key_order, key_slots, key_start, key_turn = jax.random.split(block_key, 4)
    token_order = jax.random.permutation(key_order, TOK_DEV).astype(jnp.int32)
    position = jnp.zeros((TOK_DEV,), jnp.int32).at[token_order].set(jnp.arange(TOK_DEV, dtype=jnp.int32))
    favored_slots = jnp.concatenate([jax.random.permutation(key_slots, CAP).astype(jnp.int32), jnp.zeros((TOK_DEV - CAP,), jnp.int32)])
    is_favored = (jnp.arange(TOK_DEV, dtype=jnp.int32) < CAP).astype(jnp.int32)
    counts_rest = TOPK - is_favored
    starts = jnp.cumsum(counts_rest) - counts_rest
    others = EXPERTS - 1
    offset = jax.random.randint(key_start, (), 0, others)
    column = jnp.arange(TOPK, dtype=jnp.int32)
    rest_index = starts[:, None] + column[None, :] - is_favored[:, None]
    rest_class = (offset + rest_index) % others
    rest_expert = rest_class + (rest_class >= favored).astype(jnp.int32)
    rest_slot = rest_index // others
    head_mark = (is_favored[:, None] == 1) & (column[None, :] == 0)
    place_expert = jnp.where(head_mark, favored, rest_expert)
    place_slot = jnp.where(head_mark, favored_slots[:, None], rest_slot)
    token_expert = place_expert[position]
    token_slot = place_slot[position]
    turn_by = jax.random.randint(key_turn, (TOK_DEV,), 0, TOPK)
    column_pick = (column[None, :] + turn_by[:, None]) % TOPK
    return (jnp.take_along_axis(token_expert, column_pick, axis=1).astype(jnp.int32), jnp.take_along_axis(token_slot, column_pick, axis=1).astype(jnp.int32))


def route_table(key):
    favored = jax.random.randint(jax.random.fold_in(key, 12), (N_REPLICA,), 0, EXPERTS)
    block_favored = jnp.repeat(favored, N_EXPERT)
    block_keys = jax.random.split(jax.random.fold_in(key, 13), N_REPLICA * N_EXPERT)
    drawn_routes, drawn_slots = jax.vmap(block_table)(block_keys, block_favored)
    return (drawn_routes.reshape(TOKENS, TOPK), drawn_slots.reshape(TOKENS, TOPK))


def draw_routes(key, part):
    drawn_routes, drawn_slots = route_table(key)
    return drawn_routes


def draw_slot_index(key, part):
    drawn_routes, drawn_slots = route_table(key)
    return drawn_slots


def block_scale(stream_key, extent, pieces, low, top_value):
    def one(dim, parts):
        steps = jax.random.uniform(jax.random.fold_in(jax.random.fold_in(stream_key, 6), dim), (parts,), jnp.float32, low / len(pieces), top_value / len(pieces))
        return jnp.repeat(jnp.exp(steps), extent[dim] // parts).reshape((-1,) + (1,) * (len(extent) - dim - 1))

    level = one(*pieces[0])
    for cut in pieces[1:]:
        level = level * one(*cut)
    return level


def centred(own_key, dims, scale, bound, pieces=(), held_as=jnp.bfloat16):
    drawn = scale * jax.random.normal(own_key, dims, jnp.float32)
    if pieces:
        drawn = drawn * block_scale(own_key, dims, pieces, -0.22, 0.18)
    return jnp.clip(drawn, -bound, bound).astype(held_as)


def setup_inputs(seed: int = 0) -> dict:
    arg_keys = jax.random.split(jax.random.key(seed), 12)
    return {
        "tokens": centred(arg_keys[0], (TOKENS, D), 1.0, 6.0, ((0, 32),)),
        "cotangent": centred(arg_keys[1], (TOKENS, D), 1.0, 6.0, ((0, 32),)),
        "routes": draw_routes(jax.random.fold_in(arg_keys[11], 71), 0),
        "slot_index": draw_slot_index(jax.random.fold_in(arg_keys[11], 71), 0),
        "route_weights": jnp.clip(jnp.exp(math.log(1.0) - 2.9957323 * jax.random.uniform(arg_keys[4], (TOKENS, TOPK), jnp.float32) ** block_scale(arg_keys[4], (TOKENS, TOPK), ((0, 32),), -0.2, 0.2)), 0.05, 1.0),
        "gate_weight": centred(arg_keys[5], (N_REPLICA, EXPERTS, D, FF), D ** -0.5, 0.125, ((0, 8), (1, 4))),
        "up_weight": centred(arg_keys[6], (N_REPLICA, EXPERTS, D, FF), D ** -0.5, 0.125, ((0, 8), (1, 4))),
        "down_weight": centred(arg_keys[7], (N_REPLICA, EXPERTS, FF, D), FF ** -0.5, 0.25, ((0, 8), (1, 4))),
        "moment_first": centred(arg_keys[8], (N_REPLICA, EXPERTS, FF, D), 1.0, 6.0, ((0, 8), (1, 4)), jnp.float32),
        "moment_second": jnp.clip(jnp.exp(math.log(20.0) - 3.6888795 * jax.random.uniform(arg_keys[9], (N_REPLICA, EXPERTS, FF, D), jnp.float32) ** block_scale(arg_keys[9], (N_REPLICA, EXPERTS, FF, D), ((0, 8), (1, 4)), -0.2, 0.2)), 0.5, 20.0),
        "step_count": jax.random.randint(arg_keys[10], (), 0, 1000).astype(jnp.int32),
    }


beta_first = 0.9
beta_second = 0.95
learn_rate = 0.01
decay_rate = 0.1
adam_eps = 1e-08

def expert_forward(expert_rows, gate_w, up_w, down_w):
    gate_act = jnp.dot(expert_rows, gate_w, preferred_element_type=jnp.float32)
    up_act = jnp.dot(expert_rows, up_w, preferred_element_type=jnp.float32)
    gate_sigmoid = jax.nn.sigmoid(gate_act)
    hidden = (gate_act * gate_sigmoid * up_act).astype(jnp.bfloat16)
    expert_out = jnp.dot(hidden, down_w, preferred_element_type=jnp.float32).astype(jnp.bfloat16)
    return (gate_act, up_act, gate_sigmoid, hidden, expert_out)

def expert_backward(grad_rows, gate_act, up_act, gate_sigmoid, hidden, gate_w, up_w, down_w):
    hidden_grad = jnp.dot(grad_rows, down_w.T, preferred_element_type=jnp.float32)
    gate_grad = (hidden_grad * up_act * gate_sigmoid * (1.0 + gate_act * (1.0 - gate_sigmoid))).astype(jnp.bfloat16)
    up_grad = (hidden_grad * gate_act * gate_sigmoid).astype(jnp.bfloat16)
    slot_grad = (jnp.dot(gate_grad, gate_w.T, preferred_element_type=jnp.float32) + jnp.dot(up_grad, up_w.T, preferred_element_type=jnp.float32)).astype(jnp.bfloat16)
    down_grad = jnp.dot(hidden.T, grad_rows, preferred_element_type=jnp.float32)
    return (slot_grad, down_grad)

def adamw_update(weight, first_moment, second_moment, gradient, step_number):
    first_new = beta_first * first_moment + (1.0 - beta_first) * gradient
    second_new = beta_second * second_moment + (1.0 - beta_second) * gradient * gradient
    first_hat = first_new / (1.0 - jnp.power(jnp.float32(beta_first), step_number))
    second_hat = second_new / (1.0 - jnp.power(jnp.float32(beta_second), step_number))
    weight_full = weight.astype(jnp.float32)
    stepped = weight_full - learn_rate * (first_hat / (jnp.sqrt(second_hat) + adam_eps) + decay_rate * weight_full)
    return (stepped.astype(jnp.bfloat16), first_new, second_new)

def fill_block(tok_block, grad_block, route_block, slot_block, weight_block):
    weighted = (weight_block[:, :, None] * grad_block[:, None, :].astype(jnp.float32)).astype(jnp.bfloat16)
    repeated = jnp.broadcast_to(tok_block[:, None, :], (TOK_DEV, TOPK, D))
    sent_tokens = jnp.zeros((EXPERTS, CAP, D), jnp.bfloat16).at[route_block, slot_block].set(repeated)
    sent_grads = jnp.zeros((EXPERTS, CAP, D), jnp.bfloat16).at[route_block, slot_block].set(weighted)
    return (sent_tokens, sent_grads)

def collect_block(back_grad, back_out, grad_block, route_block, slot_block):
    route_rows = back_grad[route_block, slot_block]
    token_grad = lax.optimization_barrier(jnp.sum(route_rows.astype(jnp.float32), axis=1)).astype(jnp.bfloat16)
    route_out = back_out[route_block, slot_block].astype(jnp.float32)
    route_grad = lax.optimization_barrier(jnp.sum(route_out * grad_block[:, None, :].astype(jnp.float32), axis=2))
    return (token_grad, route_grad)

def reference(tokens, cotangent, routes, slot_index, route_weights, gate_weight, up_weight, down_weight, moment_first, moment_second, step_count):
    step_number = (step_count + 1).astype(jnp.float32)

    def one_group(group_item):
        tok_g, grad_g, route_g, slot_g, weight_g, gate_g, up_g, down_g, first_g, second_g = group_item
        sent_tokens, sent_grads = jax.vmap(fill_block)(tok_g, grad_g, route_g, slot_g, weight_g)
        got_tokens = jnp.swapaxes(sent_tokens, 0, 1).reshape(EXPERTS, N_EXPERT * CAP, D)
        got_grads = jnp.swapaxes(sent_grads, 0, 1).reshape(EXPERTS, N_EXPERT * CAP, D)

        def one_expert(expert_item):
            token_rows, grad_rows, gate_w, up_w, down_w, first_moment, second_moment = expert_item
            gate_act, up_act, gate_sigmoid, hidden, expert_out = expert_forward(token_rows, gate_w, up_w, down_w)
            slot_grad, down_grad = expert_backward(grad_rows, gate_act, up_act, gate_sigmoid, hidden, gate_w, up_w, down_w)
            stepped, first_new, second_new = adamw_update(down_w, first_moment, second_moment, down_grad, step_number)
            return (slot_grad, expert_out, stepped, first_new, second_new)
        slot_grad, expert_out, stepped, first_new, second_new = lax.map(one_expert, (got_tokens, got_grads, gate_g, up_g, down_g, first_g, second_g))
        back_grad = jnp.swapaxes(slot_grad.reshape(EXPERTS, N_EXPERT, CAP, D), 0, 1)
        back_out = jnp.swapaxes(expert_out.reshape(EXPERTS, N_EXPERT, CAP, D), 0, 1)
        token_grad, route_grad = jax.vmap(collect_block)(back_grad, back_out, grad_g, route_g, slot_g)
        return (token_grad, route_grad, stepped, first_new, second_new)
    group_inputs = (tokens.reshape(N_REPLICA, N_EXPERT, TOK_DEV, D), cotangent.reshape(N_REPLICA, N_EXPERT, TOK_DEV, D), routes.reshape(N_REPLICA, N_EXPERT, TOK_DEV, TOPK), slot_index.reshape(N_REPLICA, N_EXPERT, TOK_DEV, TOPK), route_weights.reshape(N_REPLICA, N_EXPERT, TOK_DEV, TOPK), gate_weight, up_weight, down_weight, moment_first, moment_second)
    token_grad, route_grad, stepped, first_new, second_new = lax.map(one_group, group_inputs)
    exponents = N_REPLICA.bit_length() - 1
    distance = jnp.left_shift(jnp.int32(1), (step_count % exponents).astype(jnp.int32))
    partner = ((jnp.arange(N_REPLICA, dtype=jnp.int32) + distance) % N_REPLICA).astype(jnp.int32)
    other_weight = jnp.take(stepped, partner, axis=0)
    new_down = ((stepped.astype(jnp.float32) + other_weight.astype(jnp.float32)) * 0.5).astype(jnp.bfloat16)
    new_first = (first_new + jnp.take(first_new, partner, axis=0)) * 0.5
    new_second = (second_new + jnp.take(second_new, partner, axis=0)) * 0.5
    return (token_grad.reshape(TOKENS, D), route_grad.reshape(TOKENS, TOPK), new_down, new_first, new_second)
```

```python
from functools import partial

import jax
import jax.numpy as jnp
from jax import lax
from jax.sharding import PartitionSpec as P

beta_first = 0.9
beta_second = 0.95
learn_rate = 0.01
decay_rate = 0.1
adam_eps = 1e-08


def passed_along(block, axis, distance):
    devices = range(lax.axis_size(axis))
    route = [((i - distance) % len(devices), i) for i in devices]
    return lax.ppermute(block, axis, route)


def adamw_update(weight, first_moment, second_moment, gradient, step_number):
    first_new = beta_first * first_moment + (1.0 - beta_first) * gradient
    second_new = beta_second * second_moment + (1.0 - beta_second) * gradient * gradient
    first_hat = first_new / (1.0 - jnp.power(jnp.float32(beta_first), step_number))
    second_hat = second_new / (1.0 - jnp.power(jnp.float32(beta_second), step_number))
    weight_full = weight.astype(jnp.float32)
    stepped = weight_full - learn_rate * (
        first_hat / (jnp.sqrt(second_hat) + adam_eps) + decay_rate * weight_full
    )
    return (stepped.astype(jnp.bfloat16), first_new, second_new)


early_share = {1: 5 / 8, 2: 11 / 32}
along_second = (((1,), (1,)), ((), ()))


def early_rows(distance, rows):
    return int(rows * early_share.get(distance, 3 / 16)) // 32 * 32


def step_with(
    distance,
    tokens,
    cotangent,
    routes,
    route_weights,
    gate_w,
    up_w,
    down_w,
    moment_first,
    moment_second,
    step_number,
):
    f32, bf16 = jnp.float32, jnp.bfloat16
    tok_rows, model_width = tokens.shape
    experts = lax.axis_size("expert")
    replicas = lax.axis_size("replica")
    split = early_rows(distance, down_w.shape[0])

    def fetch(block):
        return passed_along(block, "replica", replicas - distance)

    far_first = fetch(moment_first[:split].astype(bf16))
    far_second = fetch(moment_second[:split].astype(bf16))
    far_down = fetch(down_w[:split])

    named = routes[:, :, None] == jnp.arange(experts, dtype=jnp.int32)
    sent_scale = jnp.sum(jnp.where(named, route_weights[:, :, None], 0.0), axis=1).T
    scale = lax.all_to_all(sent_scale, "expert", split_axis=0, concat_axis=0, tiled=True)
    scale = scale.reshape(-1)
    all_tokens = lax.all_gather(tokens, "expert", axis=0, tiled=True)
    all_cot = lax.all_gather(cotangent, "expert", axis=0, tiled=True)

    gate_act = jnp.dot(all_tokens, gate_w, preferred_element_type=f32)
    up_act = jnp.dot(all_tokens, up_w, preferred_element_type=f32)
    gate_sigmoid = jax.nn.sigmoid(gate_act)
    hidden = (gate_act * gate_sigmoid * up_act).astype(bf16)
    grad_rows = (scale[:, None] * all_cot.astype(f32)).astype(bf16)
    down_grad = lax.dot_general(
        hidden, grad_rows, (((0,), (0,)), ((), ())), preferred_element_type=f32
    )
    far_grad = fetch(down_grad[:split].astype(bf16))
    stepped, first_new, second_new = adamw_update(
        down_w, moment_first, moment_second, down_grad, step_number
    )
    late_down = fetch(stepped[split:])
    late_first = fetch(first_new[split:].astype(bf16))
    late_second = fetch(second_new[split:].astype(bf16))

    hidden_grad = lax.dot_general(grad_rows, down_w, along_second, preferred_element_type=f32)
    route_dot = jnp.sum(hidden.astype(f32) * hidden_grad, axis=1)
    route_dot = route_dot / jnp.where(scale > 0.0, scale, 1.0)
    back_dot = lax.all_to_all(
        route_dot.reshape(experts, tok_rows), "expert", split_axis=0, concat_axis=0, tiled=True
    )
    route_grad = jnp.sum(jnp.where(named, back_dot.T[:, None, :], 0.0), axis=2)
    gate_grad = (
        hidden_grad * up_act * gate_sigmoid * (1.0 + gate_act * (1.0 - gate_sigmoid))
    ).astype(bf16)
    up_grad = (hidden_grad * gate_act * gate_sigmoid).astype(bf16)
    slot_grad = (
        lax.dot_general(gate_grad, gate_w, along_second, preferred_element_type=f32)
        + lax.dot_general(up_grad, up_w, along_second, preferred_element_type=f32)
    ).astype(bf16)
    token_grad = lax.psum_scatter(slot_grad, "expert", scatter_dimension=0, tiled=True)

    far_stepped, far_first, far_second = adamw_update(
        far_down, far_first.astype(f32), far_second.astype(f32), far_grad.astype(f32), step_number
    )

    def half_sum(mine, early, late):
        other = jnp.concatenate([early.astype(f32), late.astype(f32)], 0)
        return (mine.astype(f32) + other) * 0.5

    new_down = half_sum(stepped, far_stepped, late_down).astype(bf16)
    new_first = half_sum(first_new, far_first, late_first)
    new_second = half_sum(second_new, far_second, late_second)
    return (token_grad, route_grad, new_down, new_first, new_second)


def shards(
    tokens,
    cotangent,
    routes,
    slot_index,
    route_weights,
    gate_weight,
    up_weight,
    down_weight,
    moment_first,
    moment_second,
    step_count,
):
    exponents = lax.axis_size("replica").bit_length() - 1
    step_number = (step_count + 1).astype(jnp.float32)
    token_grad, route_grad, new_down, new_first, new_second = lax.switch(
        step_count % exponents,
        [partial(step_with, 1 << exponent) for exponent in range(exponents)],
        tokens,
        cotangent,
        routes,
        route_weights,
        gate_weight[0, 0],
        up_weight[0, 0],
        down_weight[0, 0],
        moment_first[0, 0],
        moment_second[0, 0],
        step_number,
    )
    return (
        token_grad,
        route_grad,
        new_down[None, None],
        new_first[None, None],
        new_second[None, None],
    )


def solution(mesh):
    placed = (
        P(("replica", "expert"), None),
        P(("replica", "expert"), None),
        P(("replica", "expert"), None),
        P(("replica", "expert"), None),
        P(("replica", "expert"), None),
        P("replica", "expert", None, None),
        P("replica", "expert", None, None),
        P("replica", "expert", None, None),
        P("replica", "expert", None, None),
        P("replica", "expert", None, None),
        P(),
    )
    return jax.shard_map(
        shards,
        mesh=mesh,
        in_specs=placed,
        out_specs=(
            P(("replica", "expert"), None),
            P(("replica", "expert"), None),
            P("replica", "expert", None, None),
            P("replica", "expert", None, None),
            P("replica", "expert", None, None),
        ),
        check_vma=False,
    )
```

```python
from functools import partial

import jax
import jax.numpy as jnp
from jax import lax
from jax.experimental import pallas as pl
from jax.experimental.pallas import tpu as pltpu
from jax.sharding import PartitionSpec as P

beta_first = 0.9
beta_second = 0.95
learn_rate = 0.01
decay_rate = 0.1
adam_eps = 1e-08


def passed_along(block, axis, distance):
    devices = range(lax.axis_size(axis))
    route = [((i - distance) % len(devices), i) for i in devices]
    return lax.ppermute(block, axis, route)


def adamw_update(weight, first_moment, second_moment, gradient, step_number):
    first_new = beta_first * first_moment + (1.0 - beta_first) * gradient
    second_new = beta_second * second_moment + (1.0 - beta_second) * gradient * gradient
    first_hat = first_new / (1.0 - jnp.power(jnp.float32(beta_first), step_number))
    second_hat = second_new / (1.0 - jnp.power(jnp.float32(beta_second), step_number))
    weight_full = weight.astype(jnp.float32)
    stepped = weight_full - learn_rate * (
        first_hat / (jnp.sqrt(second_hat) + adam_eps) + decay_rate * weight_full
    )
    return (stepped.astype(jnp.bfloat16), first_new, second_new)


early_share = {1: 5 / 8, 2: 11 / 32}
along_second = (((1,), (1,)), ((), ()))


def early_rows(distance, rows):
    return int(rows * early_share.get(distance, 3 / 16)) // 32 * 32


def plane_kernel(
    tok_ref,
    cot_ref,
    gate_hbm,
    up_hbm,
    gate_out,
    up_out,
    cot_out,
    tok_buf,
    gate_w,
    up_w,
    send_sem,
    recv_sem,
    load_sem,
):
    rows = tok_ref.shape[0]
    half = rows // 2
    me = lax.axis_index("expert")
    beside = me + 1 - 2 * (me % 2)
    across = (me + 2) % 4
    corner = (beside + 2) % 4

    loads = [
        pltpu.make_async_copy(gate_hbm, gate_w, load_sem.at[0]),
        pltpu.make_async_copy(up_hbm, up_w, load_sem.at[1]),
        pltpu.make_async_copy(cot_ref, cot_out.at[pl.ds(me * rows, rows)], load_sem.at[2]),
    ]
    for load in loads:
        load.start()

    barrier = pltpu.get_barrier_semaphore()
    for other in (beside, across):
        pl.semaphore_signal(
            barrier, inc=1, device_id={"expert": other}, device_id_type=pl.DeviceIdType.MESH
        )
    pl.semaphore_wait(barrier, 2)

    def send(source, target, origin, part, array, slot, to):
        return pltpu.make_async_remote_copy(
            src_ref=source,
            dst_ref=target.at[pl.ds(origin * rows + part * half, half)],
            send_sem=send_sem.at[array, slot],
            recv_sem=recv_sem.at[array, slot],
            device_id={"expert": to},
            device_id_type=pl.DeviceIdType.MESH,
        )

    def own(array, source, target):
        copies = [
            send(source.at[pl.ds(0, half)], target, me, 0, array, 0, beside),
            send(source.at[pl.ds(half, half)], target, me, 1, array, 1, across),
            send(source.at[pl.ds(half, half)], target, me, 1, array, 2, beside),
            send(source.at[pl.ds(0, half)], target, me, 0, array, 3, across),
        ]
        for copy in copies:
            copy.start()
        return copies

    def forward(array, target, copies):
        copies[0].wait_recv()
        first = target.at[pl.ds(beside * rows, half)]
        onward = send(first, target, beside, 0, array, 4, across)
        onward.start()
        copies[1].wait_recv()
        second = target.at[pl.ds(across * rows + half, half)]
        sideways = send(second, target, across, 1, array, 5, beside)
        sideways.start()
        return copies + [onward, sideways]

    def project(block, origin):
        width = 256

        @pl.loop(0, gate_w.shape[1] // width)
        def _(tile):
            columns = pl.ds(pl.multiple_of(tile * width, width), width)
            lines = pl.ds(origin * rows, rows)
            gate_out[lines, columns] = jnp.dot(
                block[...], gate_w[:, columns], preferred_element_type=jnp.float32
            )
            up_out[lines, columns] = jnp.dot(
                block[...], up_w[:, columns], preferred_element_type=jnp.float32
            )

    tok_copies = own(0, tok_ref, tok_buf)
    tok_copies = forward(0, tok_buf, tok_copies)
    cot_copies = own(1, cot_ref, cot_out)
    loads[0].wait()
    loads[1].wait()
    project(tok_ref, me)
    tok_copies[2].wait_recv()
    project(tok_buf.at[pl.ds(beside * rows, rows)], beside)
    tok_copies[3].wait_recv()
    project(tok_buf.at[pl.ds(across * rows, rows)], across)
    cot_copies = forward(1, cot_out, cot_copies)
    tok_copies[4].wait_recv()
    tok_copies[5].wait_recv()
    project(tok_buf.at[pl.ds(corner * rows, rows)], corner)
    for copy in cot_copies[2:]:
        copy.wait_recv()
    loads[2].wait()
    for copy in tok_copies + cot_copies:
        copy.wait_send()


def gathered(tokens, cotangent, gate_w, up_w, collective_id):
    experts = lax.axis_size("expert")
    rows, width = tokens.shape
    total = experts * rows
    hidden_width = gate_w.shape[1]
    if experts != 4:
        all_tokens = lax.all_gather(tokens, "expert", axis=0, tiled=True)
        all_cot = lax.all_gather(cotangent, "expert", axis=0, tiled=True)
        gate_act = jnp.dot(all_tokens, gate_w, preferred_element_type=jnp.float32)
        up_act = jnp.dot(all_tokens, up_w, preferred_element_type=jnp.float32)
        return gate_act, up_act, all_cot
    in_vmem = pl.BlockSpec(memory_space=pltpu.VMEM)
    anywhere = pl.BlockSpec(memory_space=pl.ANY)
    return pl.pallas_call(
        plane_kernel,
        out_shape=(
            jax.ShapeDtypeStruct((total, hidden_width), jnp.float32),
            jax.ShapeDtypeStruct((total, hidden_width), jnp.float32),
            jax.ShapeDtypeStruct((total, width), cotangent.dtype),
        ),
        in_specs=[in_vmem, in_vmem, anywhere, anywhere],
        out_specs=(in_vmem, in_vmem, in_vmem),
        scratch_shapes=[
            pltpu.VMEM((total, width), tokens.dtype),
            pltpu.VMEM(gate_w.shape, gate_w.dtype),
            pltpu.VMEM(up_w.shape, up_w.dtype),
            pltpu.SemaphoreType.DMA((2, 6)),
            pltpu.SemaphoreType.DMA((2, 6)),
            pltpu.SemaphoreType.DMA((3,)),
        ],
        compiler_params=pltpu.CompilerParams(
            collective_id=collective_id, has_side_effects=True, vmem_limit_bytes=24 * 1024 * 1024
        ),
        cost_estimate=pl.CostEstimate(
            flops=4 * total * width * hidden_width,
            bytes_accessed=100 * 1024 * 1024,
            transcendentals=0,
        ),
    )(tokens, cotangent, gate_w, up_w)


def step_with(
    distance,
    tokens,
    cotangent,
    routes,
    route_weights,
    gate_w,
    up_w,
    down_w,
    moment_first,
    moment_second,
    step_number,
):
    f32, bf16 = jnp.float32, jnp.bfloat16
    tok_rows, model_width = tokens.shape
    experts = lax.axis_size("expert")
    replicas = lax.axis_size("replica")
    split = early_rows(distance, down_w.shape[0])

    def fetch(block):
        return passed_along(block, "replica", replicas - distance)

    far_state = fetch(
        jnp.concatenate(
            [moment_first[:split].astype(bf16), moment_second[:split].astype(bf16), down_w[:split]]
        )
    )
    far_first, far_second, far_down = (far_state[i * split : (i + 1) * split] for i in range(3))

    named = routes[:, :, None] == jnp.arange(experts, dtype=jnp.int32)
    sent_scale = jnp.sum(jnp.where(named, route_weights[:, :, None], 0.0), axis=1).T
    scale = lax.all_to_all(sent_scale, "expert", split_axis=0, concat_axis=0, tiled=True)
    scale = scale.reshape(-1)
    gate_act, up_act, all_cot = gathered(
        tokens, cotangent, gate_w, up_w, distance.bit_length() - 1
    )
    gate_sigmoid = jax.nn.sigmoid(gate_act)
    hidden = (gate_act * gate_sigmoid * up_act).astype(bf16)
    grad_rows = (scale[:, None] * all_cot.astype(f32)).astype(bf16)
    down_grad = lax.dot_general(
        hidden, grad_rows, (((0,), (0,)), ((), ())), preferred_element_type=f32
    )
    far_grad = fetch(down_grad[:split].astype(bf16))
    stepped, first_new, second_new = adamw_update(
        down_w, moment_first, moment_second, down_grad, step_number
    )
    late_down = fetch(stepped[split:])
    late_first = fetch(first_new[split:].astype(bf16))
    late_second = fetch(second_new[split:].astype(bf16))

    grad_rows, hidden, stepped, first_new, second_new = lax.optimization_barrier(
        (grad_rows, hidden, stepped, first_new, second_new)
    )
    hidden_grad = lax.dot_general(grad_rows, down_w, along_second, preferred_element_type=f32)
    route_dot = jnp.sum(hidden.astype(f32) * hidden_grad, axis=1)
    route_dot = route_dot / jnp.where(scale > 0.0, scale, 1.0)
    back_dot = lax.all_to_all(
        route_dot.reshape(experts, tok_rows), "expert", split_axis=0, concat_axis=0, tiled=True
    )
    route_grad = jnp.sum(jnp.where(named, back_dot.T[:, None, :], 0.0), axis=2)
    gate_grad = (
        hidden_grad * up_act * gate_sigmoid * (1.0 + gate_act * (1.0 - gate_sigmoid))
    ).astype(bf16)
    up_grad = (hidden_grad * gate_act * gate_sigmoid).astype(bf16)
    slot_grad = (
        lax.dot_general(gate_grad, gate_w, along_second, preferred_element_type=f32)
        + lax.dot_general(up_grad, up_w, along_second, preferred_element_type=f32)
    ).astype(bf16)
    token_grad = lax.psum_scatter(slot_grad, "expert", scatter_dimension=0, tiled=True)

    far_stepped, far_first, far_second = adamw_update(
        far_down, far_first.astype(f32), far_second.astype(f32), far_grad.astype(f32), step_number
    )

    def half_sum(mine, early, late):
        other = jnp.concatenate([early.astype(f32), late.astype(f32)], 0)
        return (mine.astype(f32) + other) * 0.5

    new_down = half_sum(stepped, far_stepped, late_down).astype(bf16)
    new_first = half_sum(first_new, far_first, late_first)
    new_second = half_sum(second_new, far_second, late_second)
    return (token_grad, route_grad, new_down, new_first, new_second)


def shards(
    tokens,
    cotangent,
    routes,
    slot_index,
    route_weights,
    gate_weight,
    up_weight,
    down_weight,
    moment_first,
    moment_second,
    step_count,
):
    exponents = lax.axis_size("replica").bit_length() - 1
    step_number = (step_count + 1).astype(jnp.float32)
    token_grad, route_grad, new_down, new_first, new_second = lax.switch(
        step_count % exponents,
        [partial(step_with, 1 << exponent) for exponent in range(exponents)],
        tokens,
        cotangent,
        routes,
        route_weights,
        gate_weight[0, 0],
        up_weight[0, 0],
        down_weight[0, 0],
        moment_first[0, 0],
        moment_second[0, 0],
        step_number,
    )
    return (
        token_grad,
        route_grad,
        new_down[None, None],
        new_first[None, None],
        new_second[None, None],
    )


def solution(mesh):
    placed = (
        P(("replica", "expert"), None),
        P(("replica", "expert"), None),
        P(("replica", "expert"), None),
        P(("replica", "expert"), None),
        P(("replica", "expert"), None),
        P("replica", "expert", None, None),
        P("replica", "expert", None, None),
        P("replica", "expert", None, None),
        P("replica", "expert", None, None),
        P("replica", "expert", None, None),
        P(),
    )
    return jax.shard_map(
        shards,
        mesh=mesh,
        in_specs=placed,
        out_specs=(
            P(("replica", "expert"), None),
            P(("replica", "expert"), None),
            P("replica", "expert", None, None),
            P("replica", "expert", None, None),
            P("replica", "expert", None, None),
        ),
        check_vma=False,
    )
```

```python
from functools import partial

import jax
import jax.numpy as jnp
from jax import lax
from jax.experimental import pallas as pl
from jax.experimental.pallas import tpu as pltpu
from jax.sharding import PartitionSpec as P

beta_first = 0.9
beta_second = 0.95
learn_rate = 0.01
decay_rate = 0.1
adam_eps = 1e-08


def passed_along(block, axis, distance):
    devices = range(lax.axis_size(axis))
    route = [((i - distance) % len(devices), i) for i in devices]
    return lax.ppermute(block, axis, route)


def adamw_update(weight, first_moment, second_moment, gradient, step_number):
    first_new = beta_first * first_moment + (1.0 - beta_first) * gradient
    second_new = beta_second * second_moment + (1.0 - beta_second) * gradient * gradient
    first_hat = first_new / (1.0 - jnp.power(jnp.float32(beta_first), step_number))
    second_hat = second_new / (1.0 - jnp.power(jnp.float32(beta_second), step_number))
    weight_full = weight.astype(jnp.float32)
    stepped = weight_full - learn_rate * (
        first_hat / (jnp.sqrt(second_hat) + adam_eps) + decay_rate * weight_full
    )
    return (stepped.astype(jnp.bfloat16), first_new, second_new)


early_share = {1: 11 / 16, 2: 7 / 16}
along_second = (((1,), (1,)), ((), ()))


def early_rows(distance, rows):
    return int(rows * early_share.get(distance, 1 / 4)) // 32 * 32


def plane_kernel(
    tok_ref,
    cot_ref,
    scale_ref,
    gate_hbm,
    up_hbm,
    gate_out,
    up_out,
    cot_out,
    scale_out,
    tok_buf,
    gate_w,
    up_w,
    send_sem,
    recv_sem,
    load_sem,
    scale_send,
    scale_recv,
):
    rows = tok_ref.shape[0]
    half = rows // 2
    me = lax.axis_index("expert")
    beside = me + 1 - 2 * (me % 2)
    across = (me + 2) % 4
    corner = (beside + 2) % 4

    loads = [
        pltpu.make_async_copy(gate_hbm, gate_w, load_sem.at[0]),
        pltpu.make_async_copy(up_hbm, up_w, load_sem.at[1]),
        pltpu.make_async_copy(cot_ref, cot_out.at[pl.ds(me * rows, rows)], load_sem.at[2]),
    ]
    for load in loads:
        load.start()

    barrier = pltpu.get_barrier_semaphore()
    for other in (beside, across, corner):
        pl.semaphore_signal(
            barrier, inc=1, device_id={"expert": other}, device_id_type=pl.DeviceIdType.MESH
        )
    pl.semaphore_wait(barrier, 3)

    def send(source, target, origin, part, array, slot, to):
        return pltpu.make_async_remote_copy(
            src_ref=source,
            dst_ref=target.at[pl.ds(origin * rows + part * half, half)],
            send_sem=send_sem.at[array, slot],
            recv_sem=recv_sem.at[array, slot],
            device_id={"expert": to},
            device_id_type=pl.DeviceIdType.MESH,
        )

    def own(array, source, target):
        copies = [
            send(source.at[pl.ds(0, half)], target, me, 0, array, 0, beside),
            send(source.at[pl.ds(half, half)], target, me, 1, array, 1, across),
            send(source.at[pl.ds(half, half)], target, me, 1, array, 2, beside),
            send(source.at[pl.ds(0, half)], target, me, 0, array, 3, across),
        ]
        for copy in copies:
            copy.start()
        return copies

    def forward(array, target, copies):
        copies[0].wait_recv()
        first = target.at[pl.ds(beside * rows, half)]
        onward = send(first, target, beside, 0, array, 4, across)
        onward.start()
        copies[1].wait_recv()
        second = target.at[pl.ds(across * rows + half, half)]
        sideways = send(second, target, across, 1, array, 5, beside)
        sideways.start()
        return copies + [onward, sideways]

    def project(block, origin):
        width = 256

        @pl.loop(0, gate_w.shape[1] // width)
        def _(tile):
            columns = pl.ds(pl.multiple_of(tile * width, width), width)
            lines = pl.ds(origin * rows, rows)
            gate_out[lines, columns] = jnp.dot(
                block[...], gate_w[:, columns], preferred_element_type=jnp.float32
            )
            up_out[lines, columns] = jnp.dot(
                block[...], up_w[:, columns], preferred_element_type=jnp.float32
            )

    tok_copies = own(0, tok_ref, tok_buf)
    scale_copies = [
        pltpu.make_async_remote_copy(
            src_ref=scale_ref,
            dst_ref=scale_out.at[me],
            send_sem=scale_send.at[slot],
            recv_sem=scale_recv.at[slot],
            device_id={"expert": to},
            device_id_type=pl.DeviceIdType.MESH,
        )
        for slot, to in enumerate((beside, across, corner))
    ]
    for copy in scale_copies:
        copy.start()
    scale_out[me] = scale_ref[...]
    tok_copies = forward(0, tok_buf, tok_copies)
    cot_copies = own(1, cot_ref, cot_out)
    loads[0].wait()
    loads[1].wait()
    project(tok_ref, me)
    tok_copies[2].wait_recv()
    project(tok_buf.at[pl.ds(beside * rows, rows)], beside)
    tok_copies[3].wait_recv()
    project(tok_buf.at[pl.ds(across * rows, rows)], across)
    cot_copies = forward(1, cot_out, cot_copies)
    tok_copies[4].wait_recv()
    tok_copies[5].wait_recv()
    project(tok_buf.at[pl.ds(corner * rows, rows)], corner)
    for copy in cot_copies[2:]:
        copy.wait_recv()
    loads[2].wait()
    for copy in scale_copies:
        copy.wait_recv()
    for copy in tok_copies + cot_copies + scale_copies:
        copy.wait_send()


def gathered(tokens, cotangent, sent_scale, gate_w, up_w, collective_id):
    experts = lax.axis_size("expert")
    rows, width = tokens.shape
    total = experts * rows
    hidden_width = gate_w.shape[1]
    if experts != 4:
        all_tokens = lax.all_gather(tokens, "expert", axis=0, tiled=True)
        all_cot = lax.all_gather(cotangent, "expert", axis=0, tiled=True)
        gate_act = jnp.dot(all_tokens, gate_w, preferred_element_type=jnp.float32)
        up_act = jnp.dot(all_tokens, up_w, preferred_element_type=jnp.float32)
        all_scale = lax.all_gather(sent_scale, "expert", axis=0, tiled=False)
        return gate_act, up_act, all_cot, all_scale
    in_vmem = pl.BlockSpec(memory_space=pltpu.VMEM)
    anywhere = pl.BlockSpec(memory_space=pl.ANY)
    return pl.pallas_call(
        plane_kernel,
        out_shape=(
            jax.ShapeDtypeStruct((total, hidden_width), jnp.float32),
            jax.ShapeDtypeStruct((total, hidden_width), jnp.float32),
            jax.ShapeDtypeStruct((total, width), cotangent.dtype),
            jax.ShapeDtypeStruct((experts,) + sent_scale.shape, sent_scale.dtype),
        ),
        in_specs=[in_vmem, in_vmem, in_vmem, anywhere, anywhere],
        out_specs=(in_vmem, in_vmem, in_vmem, in_vmem),
        scratch_shapes=[
            pltpu.VMEM((total, width), tokens.dtype),
            pltpu.VMEM(gate_w.shape, gate_w.dtype),
            pltpu.VMEM(up_w.shape, up_w.dtype),
            pltpu.SemaphoreType.DMA((2, 6)),
            pltpu.SemaphoreType.DMA((2, 6)),
            pltpu.SemaphoreType.DMA((3,)),
            pltpu.SemaphoreType.DMA((3,)),
            pltpu.SemaphoreType.DMA((3,)),
        ],
        compiler_params=pltpu.CompilerParams(
            collective_id=collective_id, has_side_effects=True, vmem_limit_bytes=24 * 1024 * 1024
        ),
        cost_estimate=pl.CostEstimate(
            flops=4 * total * width * hidden_width,
            bytes_accessed=100 * 1024 * 1024,
            transcendentals=0,
        ),
    )(tokens, cotangent, sent_scale, gate_w, up_w)


def step_with(
    distance,
    tokens,
    cotangent,
    routes,
    route_weights,
    gate_w,
    up_w,
    down_w,
    moment_first,
    moment_second,
    step_number,
):
    f32, bf16 = jnp.float32, jnp.bfloat16
    tok_rows, model_width = tokens.shape
    experts = lax.axis_size("expert")
    replicas = lax.axis_size("replica")
    split = early_rows(distance, down_w.shape[0])

    def fetch(block):
        return passed_along(block, "replica", replicas - distance)

    far_first = fetch(moment_first[:split].astype(bf16))
    far_second = fetch(moment_second[:split].astype(bf16))
    far_down = fetch(down_w[:split])

    named = routes[:, :, None] == jnp.arange(experts, dtype=jnp.int32)
    sent_scale = jnp.sum(jnp.where(named, route_weights[:, :, None], 0.0), axis=1).T
    gate_act, up_act, all_cot, all_scale = gathered(
        tokens, cotangent, sent_scale, gate_w, up_w, distance.bit_length() - 1
    )
    scale = lax.dynamic_index_in_dim(all_scale, lax.axis_index("expert"), 1, keepdims=False)
    scale = scale.reshape(-1)

    gate_sigmoid = jax.nn.sigmoid(gate_act)
    hidden = (gate_act * gate_sigmoid * up_act).astype(bf16)
    grad_rows = (scale[:, None] * all_cot.astype(f32)).astype(bf16)

    def grad_of(columns):
        along_first = (((0,), (0,)), ((), ()))
        return lax.dot_general(columns, grad_rows, along_first, preferred_element_type=f32)

    late_grad = grad_of(hidden[:, split:])
    late_mine = adamw_update(
        down_w[split:], moment_first[split:], moment_second[split:], late_grad, step_number
    )
    late_first = fetch(late_mine[1].astype(bf16))
    late_second = fetch(late_mine[2].astype(bf16))
    late_down = fetch(late_mine[0])
    early_grad = grad_of(hidden[:, :split])
    far_grad = fetch(early_grad.astype(bf16))
    early_mine = adamw_update(
        down_w[:split], moment_first[:split], moment_second[:split], early_grad, step_number
    )

    grad_rows, hidden, late_mine, early_grad = lax.optimization_barrier(
        (grad_rows, hidden, late_mine, early_grad)
    )
    hidden_grad = lax.dot_general(grad_rows, down_w, along_second, preferred_element_type=f32)
    route_dot = jnp.sum(hidden.astype(f32) * hidden_grad, axis=1)
    route_dot = route_dot / jnp.where(scale > 0.0, scale, 1.0)
    back_dot = lax.all_to_all(
        route_dot.reshape(experts, tok_rows), "expert", split_axis=0, concat_axis=0, tiled=True
    )
    route_grad = jnp.sum(jnp.where(named, back_dot.T[:, None, :], 0.0), axis=2)
    gate_grad = (
        hidden_grad * up_act * gate_sigmoid * (1.0 + gate_act * (1.0 - gate_sigmoid))
    ).astype(bf16)
    up_grad = (hidden_grad * gate_act * gate_sigmoid).astype(bf16)
    slot_grad = (
        lax.dot_general(gate_grad, gate_w, along_second, preferred_element_type=f32)
        + lax.dot_general(up_grad, up_w, along_second, preferred_element_type=f32)
    ).astype(bf16)
    token_grad = lax.psum_scatter(slot_grad, "expert", scatter_dimension=0, tiled=True)

    far_mine = adamw_update(
        far_down, far_first.astype(f32), far_second.astype(f32), far_grad.astype(f32), step_number
    )

    def half_sum(mine, other):
        return (mine.astype(f32) + other.astype(f32)) * 0.5

    early = [half_sum(mine, other) for mine, other in zip(early_mine, far_mine)]
    late = [
        half_sum(mine, other)
        for mine, other in zip(late_mine, (late_down, late_first, late_second))
    ]
    new_down, new_first, new_second = (jnp.concatenate(pair, 0) for pair in zip(early, late))
    new_down = new_down.astype(bf16)
    return (token_grad, route_grad, new_down, new_first, new_second)


def shards(
    tokens,
    cotangent,
    routes,
    slot_index,
    route_weights,
    gate_weight,
    up_weight,
    down_weight,
    moment_first,
    moment_second,
    step_count,
):
    exponents = lax.axis_size("replica").bit_length() - 1
    step_number = (step_count + 1).astype(jnp.float32)
    token_grad, route_grad, new_down, new_first, new_second = lax.switch(
        step_count % exponents,
        [partial(step_with, 1 << exponent) for exponent in range(exponents)],
        tokens,
        cotangent,
        routes,
        route_weights,
        gate_weight[0, 0],
        up_weight[0, 0],
        down_weight[0, 0],
        moment_first[0, 0],
        moment_second[0, 0],
        step_number,
    )
    return (
        token_grad,
        route_grad,
        new_down[None, None],
        new_first[None, None],
        new_second[None, None],
    )


def solution(mesh):
    placed = (
        P(("replica", "expert"), None),
        P(("replica", "expert"), None),
        P(("replica", "expert"), None),
        P(("replica", "expert"), None),
        P(("replica", "expert"), None),
        P("replica", "expert", None, None),
        P("replica", "expert", None, None),
        P("replica", "expert", None, None),
        P("replica", "expert", None, None),
        P("replica", "expert", None, None),
        P(),
    )
    return jax.shard_map(
        shards,
        mesh=mesh,
        in_specs=placed,
        out_specs=(
            P(("replica", "expert"), None),
            P(("replica", "expert"), None),
            P("replica", "expert", None, None),
            P("replica", "expert", None, None),
            P("replica", "expert", None, None),
        ),
        check_vma=False,
    )
```

```python
from functools import partial

import jax
import jax.numpy as jnp
from jax import lax
from jax.experimental import pallas as pl
from jax.experimental.pallas import tpu as pltpu
from jax.sharding import PartitionSpec as P

beta_first = 0.9
beta_second = 0.95
learn_rate = 0.01
decay_rate = 0.1
adam_eps = 1e-08


def passed_along(block, axis, distance):
    devices = range(lax.axis_size(axis))
    route = [((i - distance) % len(devices), i) for i in devices]
    return lax.ppermute(block, axis, route)


def adamw_update(weight, first_moment, second_moment, gradient, step_number):
    first_new = beta_first * first_moment + (1.0 - beta_first) * gradient
    second_new = beta_second * second_moment + (1.0 - beta_second) * gradient * gradient
    first_hat = first_new / (1.0 - jnp.power(jnp.float32(beta_first), step_number))
    second_hat = second_new / (1.0 - jnp.power(jnp.float32(beta_second), step_number))
    weight_full = weight.astype(jnp.float32)
    stepped = weight_full - learn_rate * (
        first_hat / (jnp.sqrt(second_hat) + adam_eps) + decay_rate * weight_full
    )
    return (stepped.astype(jnp.bfloat16), first_new, second_new)


early_share = {1: 5 / 8, 2: 3 / 8}
along_second = (((1,), (1,)), ((), ()))


def early_rows(distance, rows):
    return int(rows * early_share.get(distance, 7 / 32)) // 16 * 16


def plane_kernel(
    tok_ref,
    cot_ref,
    scale_ref,
    gate_hbm,
    up_hbm,
    gate_out,
    up_out,
    cot_out,
    scale_out,
    tok_buf,
    gate_w,
    up_w,
    send_sem,
    recv_sem,
    load_sem,
    scale_send,
    scale_recv,
):
    rows = tok_ref.shape[0]
    half = rows // 2
    me = lax.axis_index("expert")
    beside = me + 1 - 2 * (me % 2)
    across = (me + 2) % 4
    corner = (beside + 2) % 4

    loads = [
        pltpu.make_async_copy(gate_hbm, gate_w, load_sem.at[0]),
        pltpu.make_async_copy(up_hbm, up_w, load_sem.at[1]),
        pltpu.make_async_copy(cot_ref, cot_out.at[pl.ds(me * rows, rows)], load_sem.at[2]),
    ]
    for load in loads:
        load.start()

    barrier = pltpu.get_barrier_semaphore()
    for other in (beside, across, corner):
        pl.semaphore_signal(
            barrier, inc=1, device_id={"expert": other}, device_id_type=pl.DeviceIdType.MESH
        )
    pl.semaphore_wait(barrier, 3)

    def send(source, target, origin, part, array, slot, to):
        return pltpu.make_async_remote_copy(
            src_ref=source,
            dst_ref=target.at[pl.ds(origin * rows + part * half, half)],
            send_sem=send_sem.at[array, slot],
            recv_sem=recv_sem.at[array, slot],
            device_id={"expert": to},
            device_id_type=pl.DeviceIdType.MESH,
        )

    def own(array, source, target):
        copies = [
            send(source.at[pl.ds(0, half)], target, me, 0, array, 0, beside),
            send(source.at[pl.ds(half, half)], target, me, 1, array, 1, across),
            send(source.at[pl.ds(half, half)], target, me, 1, array, 2, beside),
            send(source.at[pl.ds(0, half)], target, me, 0, array, 3, across),
        ]
        for copy in copies:
            copy.start()
        return copies

    def forward(array, target, copies):
        copies[0].wait_recv()
        first = target.at[pl.ds(beside * rows, half)]
        onward = send(first, target, beside, 0, array, 4, across)
        onward.start()
        copies[1].wait_recv()
        second = target.at[pl.ds(across * rows + half, half)]
        sideways = send(second, target, across, 1, array, 5, beside)
        sideways.start()
        return copies + [onward, sideways]

    def project(block, origin):
        width = 256

        @pl.loop(0, gate_w.shape[1] // width)
        def _(tile):
            columns = pl.ds(pl.multiple_of(tile * width, width), width)
            lines = pl.ds(origin * rows, rows)
            gate_out[lines, columns] = jnp.dot(
                block[...], gate_w[:, columns], preferred_element_type=jnp.float32
            )
            up_out[lines, columns] = jnp.dot(
                block[...], up_w[:, columns], preferred_element_type=jnp.float32
            )

    tok_copies = own(0, tok_ref, tok_buf)
    scale_copies = [
        pltpu.make_async_remote_copy(
            src_ref=scale_ref,
            dst_ref=scale_out.at[me],
            send_sem=scale_send.at[slot],
            recv_sem=scale_recv.at[slot],
            device_id={"expert": to},
            device_id_type=pl.DeviceIdType.MESH,
        )
        for slot, to in enumerate((beside, across, corner))
    ]
    for copy in scale_copies:
        copy.start()
    scale_out[me] = scale_ref[...]
    tok_copies = forward(0, tok_buf, tok_copies)
    cot_copies = own(1, cot_ref, cot_out)
    loads[0].wait()
    loads[1].wait()
    project(tok_ref, me)
    tok_copies[2].wait_recv()
    project(tok_buf.at[pl.ds(beside * rows, rows)], beside)
    tok_copies[3].wait_recv()
    project(tok_buf.at[pl.ds(across * rows, rows)], across)
    cot_copies = forward(1, cot_out, cot_copies)
    tok_copies[4].wait_recv()
    tok_copies[5].wait_recv()
    project(tok_buf.at[pl.ds(corner * rows, rows)], corner)
    for copy in cot_copies[2:]:
        copy.wait_recv()
    loads[2].wait()
    for copy in scale_copies:
        copy.wait_recv()
    for copy in tok_copies + cot_copies + scale_copies:
        copy.wait_send()


def gathered(tokens, cotangent, sent_scale, gate_w, up_w, collective_id):
    experts = lax.axis_size("expert")
    rows, width = tokens.shape
    total = experts * rows
    hidden_width = gate_w.shape[1]
    if experts != 4:
        all_tokens = lax.all_gather(tokens, "expert", axis=0, tiled=True)
        all_cot = lax.all_gather(cotangent, "expert", axis=0, tiled=True)
        gate_act = jnp.dot(all_tokens, gate_w, preferred_element_type=jnp.float32)
        up_act = jnp.dot(all_tokens, up_w, preferred_element_type=jnp.float32)
        all_scale = lax.all_gather(sent_scale, "expert", axis=0, tiled=False)
        return gate_act, up_act, all_cot, all_scale
    in_vmem = pl.BlockSpec(memory_space=pltpu.VMEM)
    anywhere = pl.BlockSpec(memory_space=pl.ANY)
    return pl.pallas_call(
        plane_kernel,
        out_shape=(
            jax.ShapeDtypeStruct((total, hidden_width), jnp.float32),
            jax.ShapeDtypeStruct((total, hidden_width), jnp.float32),
            jax.ShapeDtypeStruct((total, width), cotangent.dtype),
            jax.ShapeDtypeStruct((experts,) + sent_scale.shape, sent_scale.dtype),
        ),
        in_specs=[in_vmem, in_vmem, in_vmem, anywhere, anywhere],
        out_specs=(in_vmem, in_vmem, in_vmem, in_vmem),
        scratch_shapes=[
            pltpu.VMEM((total, width), tokens.dtype),
            pltpu.VMEM(gate_w.shape, gate_w.dtype),
            pltpu.VMEM(up_w.shape, up_w.dtype),
            pltpu.SemaphoreType.DMA((2, 6)),
            pltpu.SemaphoreType.DMA((2, 6)),
            pltpu.SemaphoreType.DMA((3,)),
            pltpu.SemaphoreType.DMA((3,)),
            pltpu.SemaphoreType.DMA((3,)),
        ],
        compiler_params=pltpu.CompilerParams(
            collective_id=collective_id, has_side_effects=True, vmem_limit_bytes=24 * 1024 * 1024
        ),
        cost_estimate=pl.CostEstimate(
            flops=4 * total * width * hidden_width,
            bytes_accessed=100 * 1024 * 1024,
            transcendentals=0,
        ),
    )(tokens, cotangent, sent_scale, gate_w, up_w)


def step_with(
    distance,
    tokens,
    cotangent,
    routes,
    route_weights,
    gate_w,
    up_w,
    down_w,
    moment_first,
    moment_second,
    step_number,
):
    f32, bf16 = jnp.float32, jnp.bfloat16
    tok_rows, model_width = tokens.shape
    experts = lax.axis_size("expert")
    replicas = lax.axis_size("replica")
    split = early_rows(distance, down_w.shape[0])

    def fetch(block):
        return passed_along(block, "replica", replicas - distance)

    far_first = fetch(moment_first[:split].astype(bf16))
    far_second = fetch(moment_second[:split].astype(bf16))
    far_down = fetch(down_w[:split])

    named = routes[:, :, None] == jnp.arange(experts, dtype=jnp.int32)
    sent_scale = jnp.sum(jnp.where(named, route_weights[:, :, None], 0.0), axis=1).T
    gate_act, up_act, all_cot, all_scale = gathered(
        tokens, cotangent, sent_scale, gate_w, up_w, distance.bit_length() - 1
    )
    scale = lax.dynamic_index_in_dim(all_scale, lax.axis_index("expert"), 1, keepdims=False)
    scale = scale.reshape(-1)

    gate_sigmoid = jax.nn.sigmoid(gate_act)
    hidden = (gate_act * gate_sigmoid * up_act).astype(bf16)
    grad_rows = (scale[:, None] * all_cot.astype(f32)).astype(bf16)

    def grad_of(columns):
        along_first = (((0,), (0,)), ((), ()))
        return lax.dot_general(columns, grad_rows, along_first, preferred_element_type=f32)

    late_grad = grad_of(hidden[:, split:])
    late_mine = adamw_update(
        down_w[split:], moment_first[split:], moment_second[split:], late_grad, step_number
    )
    late_first = fetch(late_mine[1].astype(bf16))
    early_grad = grad_of(hidden[:, :split])
    far_grad = fetch(early_grad.astype(bf16))
    late_sent, far_down, far_second = lax.optimization_barrier(
        (late_mine[2].astype(bf16), far_down, far_second)
    )
    late_second = fetch(late_sent)
    late_sent, far_first = lax.optimization_barrier((late_mine[0], far_first))
    late_down = fetch(late_sent)
    early_mine = adamw_update(
        down_w[:split], moment_first[:split], moment_second[:split], early_grad, step_number
    )

    grad_rows, hidden, late_mine, early_grad = lax.optimization_barrier(
        (grad_rows, hidden, late_mine, early_grad)
    )
    hidden_grad = lax.dot_general(grad_rows, down_w, along_second, preferred_element_type=f32)
    route_dot = jnp.sum(hidden.astype(f32) * hidden_grad, axis=1)
    route_dot = route_dot / jnp.where(scale > 0.0, scale, 1.0)
    back_dot = lax.all_to_all(
        route_dot.reshape(experts, tok_rows), "expert", split_axis=0, concat_axis=0, tiled=True
    )
    route_grad = jnp.sum(jnp.where(named, back_dot.T[:, None, :], 0.0), axis=2)
    gate_grad = (
        hidden_grad * up_act * gate_sigmoid * (1.0 + gate_act * (1.0 - gate_sigmoid))
    ).astype(bf16)
    up_grad = (hidden_grad * gate_act * gate_sigmoid).astype(bf16)
    slot_grad = (
        lax.dot_general(gate_grad, gate_w, along_second, preferred_element_type=f32)
        + lax.dot_general(up_grad, up_w, along_second, preferred_element_type=f32)
    ).astype(bf16)
    token_grad = lax.psum_scatter(slot_grad, "expert", scatter_dimension=0, tiled=True)

    far_mine = adamw_update(
        far_down, far_first.astype(f32), far_second.astype(f32), far_grad.astype(f32), step_number
    )

    def half_sum(mine, other):
        return (mine.astype(f32) + other.astype(f32)) * 0.5

    early = [half_sum(mine, other) for mine, other in zip(early_mine, far_mine)]
    late = [
        half_sum(mine, other)
        for mine, other in zip(late_mine, (late_down, late_first, late_second))
    ]
    new_down, new_first, new_second = (jnp.concatenate(pair, 0) for pair in zip(early, late))
    new_down = new_down.astype(bf16)
    return (token_grad, route_grad, new_down, new_first, new_second)


def shards(
    tokens,
    cotangent,
    routes,
    slot_index,
    route_weights,
    gate_weight,
    up_weight,
    down_weight,
    moment_first,
    moment_second,
    step_count,
):
    exponents = lax.axis_size("replica").bit_length() - 1
    step_number = (step_count + 1).astype(jnp.float32)
    token_grad, route_grad, new_down, new_first, new_second = lax.switch(
        step_count % exponents,
        [partial(step_with, 1 << exponent) for exponent in range(exponents)],
        tokens,
        cotangent,
        routes,
        route_weights,
        gate_weight[0, 0],
        up_weight[0, 0],
        down_weight[0, 0],
        moment_first[0, 0],
        moment_second[0, 0],
        step_number,
    )
    return (
        token_grad,
        route_grad,
        new_down[None, None],
        new_first[None, None],
        new_second[None, None],
    )


def solution(mesh):
    placed = (
        P(("replica", "expert"), None),
        P(("replica", "expert"), None),
        P(("replica", "expert"), None),
        P(("replica", "expert"), None),
        P(("replica", "expert"), None),
        P("replica", "expert", None, None),
        P("replica", "expert", None, None),
        P("replica", "expert", None, None),
        P("replica", "expert", None, None),
        P("replica", "expert", None, None),
        P(),
    )
    return jax.shard_map(
        shards,
        mesh=mesh,
        in_specs=placed,
        out_specs=(
            P(("replica", "expert"), None),
            P(("replica", "expert"), None),
            P("replica", "expert", None, None),
            P("replica", "expert", None, None),
            P("replica", "expert", None, None),
        ),
        check_vma=False,
    )
```
